32 devices in a mesh: vocab: 16 (over z, x, core), hid: 2 (over y).
Axes of the slice: x: 2, y: 2, z: 4, core: 2. Of those that a mesh axis runs over, the one named last changes fastest.
Arguments:
- posterior: bfloat16 [128, 16384], P(None, 'vocab'), may hold values from 1.9e-09 to 1, as said below
- transition: bfloat16 [16384, 16384], P('vocab', 'hid'), may hold values from 1e-07 to 1, as said below
- emission: bfloat16 [16384, 16384], P('hid', 'vocab'), may hold values from 6e-06 to 90, as said below
- advance: bfloat16 [256, 16384], P(None, 'hid'), may hold values from 0.0099487305 to 1
- dfa_state: int32 [128], replicated, may hold values from 0 to 255
- edge_next: int32 [256, 8], replicated, may hold values from 0 to 255
- token_edge: int32 [256, 16384], P(None, 'vocab'), may hold values from 0 to 7
- allowed: int32 [128, 128], P(None, 'vocab'), may hold values from 0 to 1, as said below
Outputs:
- constrained_logprob: float32 [128, 16384], P('hid', 'vocab')
The draws below stay inside these ranges and needn't reach their ends.
Inputs may be any that keep to these rules, and one draw needn't show every extreme that they name: `allowed`: every request allows at least one block. `posterior`: positive. `transition`: positive. `emission`: positive.
All inputs are finite; a program needn't handle non-finite values.
Results may differ from the reference program's by a relative error of at most 0.0015.
Values may be sent and summed in bfloat16 or wider, within the bound.
No kernel may reach another device: no remote copies, remote signals or barrier semaphores. Data moves between devices by JAX's collectives and lax.ppermute only.
A program may use at most 128 MiB of HBM per device.

```python
import math
import jax
import jax.numpy as jnp
from jax import lax

H = 16384
V = 16384
BLK = 128
S = 256
K = 8
R = 128
NB = 128


def draw_posterior(key, part):
    logs = 2.5 * jax.random.truncated_normal(key, -4.0, 4.0, (R, H), jnp.float32) - 10.0
    return jnp.exp(logs).astype(jnp.bfloat16)


def draw_transition(key, part):
    logs = 2.0 * jax.random.truncated_normal(key, -4.0, 4.0, (H, H), jnp.float32) - 8.0
    return jnp.exp(logs).astype(jnp.bfloat16)


def draw_emission(key, part):
    boost_key = jax.random.fold_in(key, 5)
    frequency_key = jax.random.fold_in(key, 7)
    logs = 1.5 * jax.random.truncated_normal(key, -4.0, 4.0, (H, V), jnp.float32) - 6.0
    frequency = jnp.exp(jax.random.uniform(frequency_key, (V,), jnp.float32, 0.0, math.log(3.0)))
    boost_table = jnp.exp(jax.random.uniform(boost_key, (16, NB), jnp.float32, 0.0, math.log(30.0)))
    row_group = jnp.arange(H, dtype=jnp.int32) * 16 // H
    column_block = jnp.arange(V, dtype=jnp.int32) // BLK
    boost = jnp.take(jnp.take(boost_table, row_group, axis=0), column_block, axis=1)
    return (jnp.exp(logs) * frequency[None, :] * boost).astype(jnp.bfloat16)


def draw_allowed(key, part):
    coin_key = jax.random.fold_in(key, 11)
    pick_key = jax.random.fold_in(key, 23)
    coins = jax.random.randint(coin_key, (R, NB), 0, 16)
    forced = jax.random.randint(pick_key, (R, 1), 0, NB)
    blocks = jnp.arange(NB, dtype=jnp.int32)[None, :]
    return jnp.where((coins == 0) | (blocks == forced), 1, 0).astype(jnp.int32)


def set_ends(result, stream_key, smallest, high):
    spot = [jax.random.randint(jax.random.fold_in(stream_key, axis), (), 0, length) for axis, length in enumerate(result.shape)]
    main_axis = result.shape.index(max(result.shape))
    next_to = spot[:main_axis] + [(spot[main_axis] + 1) % result.shape[main_axis]] + spot[main_axis + 1:]
    return result.at[tuple(spot)].set(smallest).at[tuple(next_to)].set(high)


def block_levels(own_key, dims, split, least, largest):
    level, own = 1.0, jax.random.fold_in(own_key, 6)
    for axis_at, shards_of in split:
        draws = jnp.exp(jax.random.uniform(jax.random.fold_in(own, axis_at), (shards_of,), jnp.float32, least / len(split), largest / len(split)))
        level = level * jnp.repeat(draws, dims[axis_at] // shards_of).reshape([-1 if axis == axis_at else 1 for axis in range(len(dims))])
    return level


def setup_inputs(seed: int = 0) -> dict:
    key_of = jax.random.split(jax.random.key(seed), 9)
    return {
        "posterior": draw_posterior(jax.random.fold_in(key_of[8], 71), 0),
        "transition": draw_transition(jax.random.fold_in(key_of[8], 71), 0),
        "emission": draw_emission(jax.random.fold_in(key_of[8], 71), 0),
        "advance": jnp.clip(jnp.exp(math.log(1.0) - 4.61031033 * jax.random.uniform(key_of[3], (S, H), jnp.float32) ** block_levels(key_of[3], (S, H), ((1, 2),), -0.2, 0.2)), 0.0099487305, 1.0).astype(jnp.bfloat16),
        "dfa_state": set_ends(jax.random.randint(key_of[4], (R,), 0, S), jax.random.fold_in(key_of[4], 1), 0, S - 1).astype(jnp.int32),
        "edge_next": set_ends(jax.random.randint(key_of[5], (S, K), 0, S), jax.random.fold_in(key_of[5], 1), 0, S - 1).astype(jnp.int32),
        "token_edge": set_ends(jax.random.randint(key_of[6], (S, V), 0, K), jax.random.fold_in(key_of[6], 1), 0, K - 1).astype(jnp.int32),
        "allowed": draw_allowed(jax.random.fold_in(key_of[8], 71), 0),
    }


def request_scores(prior_rows, first_row, dfa_state, edge_next, token_edge, allowed, advance, emission):
    row_count = prior_rows.shape[0]
    states = lax.dynamic_slice_in_dim(dfa_state, first_row, row_count, 0)
    successor = jnp.take(edge_next, states, axis=0)
    look_rows = jnp.take(advance, successor, axis=0)
    weighted = (prior_rows.astype(jnp.float32)[:, None, :] * look_rows.astype(jnp.float32)).astype(jnp.bfloat16)
    slot_count = successor.shape[1]
    flattened = weighted.reshape(row_count * slot_count, weighted.shape[2])
    candidate = jnp.dot(flattened, emission, preferred_element_type=jnp.float32).reshape(row_count, slot_count, emission.shape[1])
    edge_slots = jnp.take(token_edge, states, axis=0)
    labels = jnp.arange(slot_count, dtype=jnp.int32)
    chosen = jnp.sum(jnp.where(edge_slots[:, None, :] == labels[None, :, None], candidate, jnp.float32(0.0)), axis=1)
    mask_rows = lax.dynamic_slice_in_dim(allowed, first_row, row_count, 0)
    token_mask = jnp.repeat(mask_rows, BLK, axis=1)
    return jnp.where(token_mask > 0, chosen, jnp.float32(0.0))


def reference(posterior, transition, emission, advance, dfa_state, edge_next, token_edge, allowed):
    prior = jnp.dot(posterior, transition, preferred_element_type=jnp.float32).astype(jnp.bfloat16)
    block_rows = R // 8
    stacked = prior.reshape(8, block_rows, H)
    starts = jnp.arange(8, dtype=jnp.int32) * block_rows

    def one_block(operands):
        return request_scores(operands[0], operands[1], dfa_state, edge_next, token_edge, allowed, advance, emission)

    pieces = lax.map(one_block, (stacked, starts))
    scores = pieces.reshape(R, V)
    totals = jnp.sum(scores, axis=1)
    token_mask = jnp.repeat(allowed, BLK, axis=1) > 0
    safe = jnp.where(token_mask, scores, jnp.float32(1.0))
    return jnp.where(token_mask, jnp.log(safe) - jnp.log(totals)[:, None], jnp.float32(0.0))
```

```python
import functools
import jax
import jax.numpy as jnp
from jax import lax
from jax.experimental import pallas as pl
from jax.experimental.pallas import tpu as pltpu
from jax.sharding import PartitionSpec as P

BLK = 128
BF16 = jnp.bfloat16
F32 = jnp.float32


def params(mib):
    return pltpu.CompilerParams(vmem_limit_bytes=mib << 20)


def half_product(posterior, transition, place, half, pieces, width):
    rows, depth = posterior.shape

    def kernel(place_ref, post_ref, trans_ref, out_ref):
        out_ref[0] = jnp.dot(post_ref[...], trans_ref[...], preferred_element_type=F32).astype(BF16)

    return pl.pallas_call(
        kernel,
        grid_spec=pltpu.PrefetchScalarGridSpec(
            num_scalar_prefetch=1,
            grid=(pieces,),
            in_specs=[
                pl.BlockSpec((rows, depth), lambda m, p: (0, 0)),
                pl.BlockSpec((depth, width), lambda m, p: (0, p[1 + half] * pieces + (p[0] ^ m))),
            ],
            out_specs=pl.BlockSpec((1, rows, width), lambda m, p: (m, 0, 0)),
        ),
        out_shape=jax.ShapeDtypeStruct((pieces, rows, width), BF16),
        compiler_params=params(40),
        cost_estimate=pl.CostEstimate(
            flops=2 * rows * depth * pieces * width, bytes_accessed=2 * depth * pieces * width, transcendentals=0
        ),
        name="prior_half",
    )(place, posterior, transition)


def successor_rows(onehot, advance, width):
    count, states = onehot.shape
    columns = advance.shape[1]

    def kernel(onehot_ref, adv_ref, out_ref):
        out_ref[...] = jnp.dot(onehot_ref[...], adv_ref[...], preferred_element_type=F32).astype(BF16)

    return pl.pallas_call(
        kernel,
        grid=(columns // width,),
        in_specs=[
            pl.BlockSpec((count, states), lambda i: (0, 0)),
            pl.BlockSpec((states, width), lambda i: (0, i)),
        ],
        out_specs=pl.BlockSpec((count, width), lambda i: (0, i)),
        out_shape=jax.ShapeDtypeStruct((count, columns), BF16),
        compiler_params=params(40),
        cost_estimate=pl.CostEstimate(
            flops=2 * count * states * columns, bytes_accessed=2 * columns * (count + states), transcendentals=0
        ),
        name="advance_rows",
    )(onehot, advance)


def piece_scores(pieces, places, look, emission, edges, mask, before, slots):
    count = len(pieces)
    rows, width = pieces[0].shape
    columns = emission.shape[1]
    has_before = before is not None

    def kernel(place_ref, *refs):
        piece_refs = refs[:count]
        look_ref, emit_ref, edge_ref, mask_ref = refs[count : count + 4]
        before_ref = refs[count + 4] if has_before else None
        out_ref, weighted, total = refs[-3:]
        step = pl.program_id(0)
        for j in range(count):

            @pl.when(step == j)
            def _():
                prior = piece_refs[j][...].astype(F32)
                for k in range(slots):
                    part = pl.ds(k * rows, rows)
                    weighted[part, :] = (prior * look_ref[part, :].astype(F32)).astype(BF16)

        @pl.when(step == 0)
        def _():
            total[...] = jnp.zeros_like(total)

        @pl.loop(0, slots)
        def _(k):
            part = pl.ds(k * rows, rows)
            total[part, :] += jnp.dot(weighted[part, :], emit_ref[...], preferred_element_type=F32)

        @pl.when(step == count - 1)
        def _():
            chosen = jnp.zeros((rows, columns), F32)
            for k in range(slots):
                chosen = jnp.where(edge_ref[...] == k, total[pl.ds(k * rows, rows), :], chosen)
            chosen = jnp.where(mask_ref[...] > 0, chosen, 0.0)
            out_ref[...] = chosen + before_ref[...] if has_before else chosen

    whole = lambda i, p: (0, 0)
    block = pl.BlockSpec((rows, columns), whole)
    return pl.pallas_call(
        kernel,
        grid_spec=pltpu.PrefetchScalarGridSpec(
            num_scalar_prefetch=1,
            grid=(count,),
            in_specs=[pl.BlockSpec((rows, width), whole) for _ in pieces]
            + [
                pl.BlockSpec((slots * rows, width), lambda i, p: (0, p[i])),
                pl.BlockSpec((width, columns), lambda i, p: (p[i], 0)),
                block,
                block,
            ]
            + [block] * has_before,
            out_specs=block,
            scratch_shapes=[pltpu.VMEM((slots * rows, width), BF16), pltpu.VMEM((slots * rows, columns), F32)],
        ),
        out_shape=jax.ShapeDtypeStruct((rows, columns), F32),
        compiler_params=params(44),
        cost_estimate=pl.CostEstimate(
            flops=2 * slots * rows * width * columns * count,
            bytes_accessed=2 * count * width * (slots * rows + columns),
            transcendentals=0,
        ),
        name="piece_scores",
    )(places, *pieces, look, emission, edges, mask, *([before] if has_before else []))


def body(sizes, posterior, transition, emission, advance, dfa_state, edge_next, token_edge, allowed):
    vocab_size, hid_size = sizes
    rows = posterior.shape[0]
    hidden = transition.shape[1]
    slots = edge_next.shape[1]
    me = lax.axis_index("vocab")
    core, chip = me % 2, me // 2
    chips = vocab_size // 2
    width = hidden // vocab_size
    direct = chips <= 8 and width % 128 == 0

    states = lax.broadcasted_iota(jnp.int32, (1, 1, advance.shape[0]), 2)
    successor = jnp.take(edge_next, dfa_state, axis=0, mode="clip")
    onehot = (successor.T[:, :, None] == states).astype(BF16).reshape(slots * rows, advance.shape[0])
    edges = jnp.take(token_edge, dfa_state, axis=0, mode="clip")
    mask = jnp.repeat(allowed, BLK, axis=1)

    def swap(array, bits):
        return lax.ppermute(array, "vocab", [(i, i ^ bits) for i in range(vocab_size)])

    scores = None
    if direct:
        place = jnp.stack([chip, 1 - core, core]).astype(jnp.int32)
        away = half_product(posterior, transition, place, 0, chips, width)
        came = swap(away, 1)
        kept = half_product(posterior, transition, place, 1, chips, width)
        sums = [kept[m].astype(F32) + came[m].astype(F32) for m in range(chips)]
        sent = [swap(sums[m].astype(BF16), 2 * m) for m in range(1, chips)]
        look = successor_rows(onehot, advance, 512)
        total = sums[0]
        for part in sent:
            total = total + part.astype(F32)
        own = total.astype(BF16)
        held = [own] + [swap(own, 2 * m) for m in range(1, chips)]
        for group in ([0, 1, 2], [3, 4, 5], [6, 7]):
            group = [m for m in group if m < chips]
            if not group:
                continue
            pieces = [held[m] for m in group] + [swap(held[m], 1) for m in group]
            places = jnp.stack(
                [core * chips + (chip ^ m) for m in group] + [(1 - core) * chips + (chip ^ m) for m in group]
            ).astype(jnp.int32)
            scores = piece_scores(pieces, places, look, emission, edges, mask, scores, slots)
    else:
        own = lax.psum_scatter(
            jnp.dot(posterior, transition, preferred_element_type=F32), "vocab", scatter_dimension=0, tiled=True
        ).astype(BF16)
        prior = lax.all_gather(own, "vocab", axis=0, tiled=True)
        look = successor_rows(onehot, advance, 512)
        count = hidden // 512
        pieces = [prior[:, 512 * j : 512 * (j + 1)] for j in range(count)]
        scores = piece_scores(
            pieces, jnp.arange(count, dtype=jnp.int32), look, emission, edges, mask, None, slots
        )

    sums = jnp.sum(scores, axis=1)
    local = rows // hid_size
    first = lax.axis_index("hid") * local
    if hid_size == 2:
        part = jnp.reshape(sums, (1, rows))
        part = part + lax.ppermute(part, "hid", [(0, 1), (1, 0)])
        bits = vocab_size // 2
        while bits:
            part = part + swap(part, bits)
            bits //= 2
        totals = lax.dynamic_slice_in_dim(part[0], first, local, 0)
        other = lax.dynamic_slice_in_dim(scores, local - first, local, 0).astype(BF16)
        came = lax.ppermute(other, "hid", [(0, 1), (1, 0)])
        mine = lax.dynamic_slice_in_dim(scores, first, local, 0) + came.astype(F32)
    else:
        mine = lax.psum_scatter(scores.astype(BF16), "hid", scatter_dimension=0, tiled=True).astype(F32)
        totals = lax.psum(jnp.sum(mine, axis=1), "vocab")
    token_mask = lax.dynamic_slice_in_dim(mask, first, local, 0) > 0
    safe = jnp.where(token_mask, mine, jnp.float32(1.0))
    return jnp.where(token_mask, jnp.log(safe) - jnp.log(totals)[:, None], jnp.float32(0.0))


def solution(mesh):
    in_specs = (
        P(None, "vocab"),
        P("vocab", "hid"),
        P("hid", "vocab"),
        P(None, "hid"),
        P(),
        P(),
        P(None, "vocab"),
        P(None, "vocab"),
    )
    sizes = (mesh.shape["vocab"], mesh.shape["hid"])
    return jax.shard_map(
        functools.partial(body, sizes), mesh=mesh, in_specs=in_specs, out_specs=P("hid", "vocab"), check_vma=False
    )
```

```python
import functools
import jax
import jax.numpy as jnp
from jax import lax
from jax.experimental import pallas as pl
from jax.experimental.pallas import tpu as pltpu
from jax.sharding import PartitionSpec as P

BLK = 128
GROUP = 32
UNIT = 256
BATCH = 4
CHEAP = 1 << 20
BF16 = jnp.bfloat16
F32 = jnp.float32
FAR_OTHER, FAR_SAME, NEAR_OTHER, NEAR_SAME = (5, 7), (4, 6), (1, 3), (0, 2)
ORDER = FAR_OTHER + FAR_SAME + NEAR_OTHER + NEAR_SAME


def params(mib):
    return pltpu.CompilerParams(vmem_limit_bytes=mib << 20)


def cheap():
    return pl.CostEstimate(flops=CHEAP, bytes_accessed=CHEAP, transcendentals=0)


def piece_place(chips, other, bits):
    me = lax.axis_index("vocab")
    core, chip = lax.rem(me, 2), lax.div(me, 2)
    return (1 - core if other else core) * chips + (chip ^ bits)


def transposed_dot(a, b):
    return lax.dot_general(a, b, (((0,), (0,)), ((), ())), preferred_element_type=F32)


SMEM = pl.BlockSpec(memory_space=pltpu.SMEM)
VMEM = pl.BlockSpec(memory_space=pltpu.VMEM)
HBM = pl.BlockSpec(memory_space=pltpu.HBM)


def half_product(posterior, transition, other, order, chips, width):
    rows, depth = posterior.shape
    pieces = len(order)

    def kernel(post_ref, trans_ref, out_ref, held, arrived):
        def copy(n):
            first = piece_place(chips, other, order[n])
            columns = pl.ds(pl.multiple_of(first * width, width), width)
            return pltpu.make_async_copy(trans_ref.at[:, columns], held.at[n], arrived.at[n])

        for n in range(pieces):
            copy(n).start()
        for n in range(pieces):
            copy(n).wait()
            out_ref[n] = jnp.dot(post_ref[...], held[n], preferred_element_type=F32).astype(BF16)

    return pl.pallas_call(
        kernel,
        in_specs=[VMEM, HBM],
        out_specs=VMEM,
        out_shape=jax.ShapeDtypeStruct((pieces, rows, width), BF16),
        scratch_shapes=[pltpu.VMEM((pieces, depth, width), BF16), pltpu.SemaphoreType.DMA((pieces,))],
        compiler_params=params(50),
        cost_estimate=cheap(),
        name="prior_half",
    )(posterior, transition)


def prepare(allowed, state, edge_next, token_edge, advance, tile):
    blocks, rows = allowed.shape
    states, columns = token_edge.shape
    slots = edge_next.shape[1]
    hidden = advance.shape[1]
    tiles = columns // tile
    each = tile // BLK
    seats = tiles * rows
    width = min(1024, hidden)
    steps = hidden // width
    pair = 2

    def kernel(allow_ref, state_ref, next_ref, token_ref, adv_ref, head_ref, select_ref, edge_ref, look_ref, hot, after, held, left):
        who = (lax.broadcasted_iota(jnp.int32, (states, rows), 0) == state_ref[...]).astype(F32).astype(BF16)
        allow = allow_ref[...].astype(F32)
        earlier = lax.broadcasted_iota(jnp.int32, (rows, rows), 0) < lax.broadcasted_iota(jnp.int32, (rows, rows), 1)
        earlier = earlier.astype(F32).astype(BF16)
        number = lax.broadcasted_iota(jnp.int32, (seats, rows), 0)
        taken = jnp.zeros((seats, rows), F32)
        used = jnp.int32(0)
        for t in range(tiles):
            need = allow[t * each : t * each + 1]
            for b in range(1, each):
                need = jnp.maximum(need, allow[t * each + b : t * each + b + 1])
            rank = jnp.dot(jnp.broadcast_to(need, (8, rows)).astype(BF16), earlier, preferred_element_type=F32)[0:1]
            units = (jnp.sum(need).astype(jnp.int32) + GROUP - 1) // GROUP
            seat = jnp.where(need > 0, rank.astype(jnp.int32) + used * GROUP, -1)
            taken += (number == seat).astype(F32)

            @pl.loop(0, units)
            def _(u):
                head_ref[1 + used + u] = t

            used = used + units
        head_ref[0] = used
        taken = taken.astype(BF16)
        select_ref[...] = taken
        following = transposed_dot(who, next_ref[...].astype(F32).astype(BF16))
        after[...] = jnp.dot(taken, following.astype(BF16), preferred_element_type=F32).astype(jnp.int32)
        names = lax.broadcasted_iota(jnp.int32, (GROUP, states), 1)

        def copy(c, n):
            span = pl.ds(pl.multiple_of(c * pair * UNIT, pair * UNIT), pair * UNIT)
            return pltpu.make_async_copy(held.at[n], look_ref.at[span, pl.ds(n * width, width)], left.at[n])

        chunks = (used + pair - 1) // pair

        @pl.loop(0, chunks)
        def _(c):
            for u in range(pair):
                succ = after[pl.ds(pl.multiple_of((c * pair + u) * GROUP, GROUP), GROUP), :]
                for k in range(slots):
                    hot[u * UNIT + k * GROUP : u * UNIT + (k + 1) * GROUP, :] = (
                        (names == succ[:, k : k + 1]).astype(F32).astype(BF16)
                    )
            for n in range(steps):

                @pl.when(c > 0)
                def _():
                    copy(c - 1, n).wait()

                held[n] = jnp.dot(
                    hot[...], adv_ref[:, n * width : (n + 1) * width], preferred_element_type=F32
                ).astype(BF16)
                copy(c, n).start()

        allow = allow.astype(BF16)
        token = token_ref[...].astype(F32).astype(BF16)
        slot = transposed_dot(who, token)
        block = lax.broadcasted_iota(jnp.int32, (blocks, columns), 1) // BLK
        spread = (block == lax.broadcasted_iota(jnp.int32, (blocks, columns), 0)).astype(F32).astype(BF16)
        edge_ref[...] = jnp.where(transposed_dot(allow, spread) > 0, slot, float(slots)).astype(BF16)

        @pl.when(chunks > 0)
        def _():
            for n in range(steps):
                copy(chunks - 1, n).wait()

    return pl.pallas_call(
        kernel,
        in_specs=[VMEM] * 5,
        out_specs=[SMEM, VMEM, VMEM, HBM],
        scratch_shapes=[
            pltpu.VMEM((pair * UNIT, states), BF16),
            pltpu.VMEM((seats, slots), jnp.int32),
            pltpu.VMEM((steps, pair * UNIT, width), BF16),
            pltpu.SemaphoreType.DMA((steps,)),
        ],
        out_shape=[
            jax.ShapeDtypeStruct((1 + seats // GROUP,), jnp.int32),
            jax.ShapeDtypeStruct((seats, rows), BF16),
            jax.ShapeDtypeStruct((rows, columns), BF16),
            jax.ShapeDtypeStruct((seats * slots, hidden), BF16),
        ],
        compiler_params=params(16),
        cost_estimate=cheap(),
        name="prepare",
    )(allowed, state, edge_next, token_edge, advance)


def piece_scores(arrays, places, head, select, look, emission, edges, before, slots, tile, last, local):
    each, rows, width = arrays[0].shape
    count = len(arrays) * each
    columns = emission.shape[1]
    seats = select.shape[0]
    started = before is not None

    def kernel(head_ref, *refs):
        piece_refs = refs[: len(arrays)]
        select_ref, look_ref, emit_ref, edge_ref = refs[len(arrays) : len(arrays) + 4]
        before_ref = refs[len(arrays) + 4] if started else None
        looks, prior, total, arrived = refs[-4:]
        outs = refs[len(arrays) + 4 + started : -4]
        units = head_ref[0]
        deep = [pl.ds(pl.multiple_of(place * width, width), width) for place in places()]

        def look_copy(i, c, u):
            here = pl.ds(pl.multiple_of((c * BATCH + u) * UNIT, UNIT), UNIT)
            return pltpu.make_async_copy(look_ref.at[here, deep[i]], looks.at[i, u], arrived.at[i, u])

        if last:
            total[...] = jnp.zeros_like(total)

        @pl.loop(0, (units + BATCH - 1) // BATCH)
        def _(c):
            here = jnp.minimum(units - c * BATCH, BATCH)

            @pl.loop(0, here)
            def _(u):
                for i in range(count):
                    look_copy(i, c, u).start()

            span = pl.ds(pl.multiple_of(c * BATCH * GROUP, BATCH * GROUP), BATCH * GROUP)
            for i in range(count):
                prior[i] = jnp.dot(
                    select_ref[span, :], piece_refs[i // each][i % each], preferred_element_type=F32
                ).astype(BF16)

            @pl.loop(0, here)
            def _(u):
                at = pl.multiple_of(head_ref[1 + c * BATCH + u] * tile, tile)
                span = pl.ds(pl.multiple_of((c * BATCH + u) * GROUP, GROUP), GROUP)
                seat = pl.ds(pl.multiple_of(u * GROUP, GROUP), GROUP)
                for i in range(count):
                    look_copy(i, c, u).wait()
                values = None
                for i in range(count):
                    rowed = looks[i, u].reshape(slots, GROUP, width)
                    weighted = (rowed * prior[i, seat, :][None]).reshape(UNIT, width)
                    part = jnp.dot(weighted, emit_ref[deep[i], pl.ds(at, tile)], preferred_element_type=F32)
                    values = part if values is None else values + part
                own = select_ref[span, :]
                edge = jnp.dot(own, edge_ref[:, pl.ds(at, tile)], preferred_element_type=F32)
                chosen = before_ref[span, :] if started else jnp.zeros((GROUP, tile), F32)
                for k in range(slots):
                    chosen += jnp.where(edge == k, values[k * GROUP : (k + 1) * GROUP], 0.0)
                if not last:
                    outs[0][span, :] = chosen
                    return
                spread = jnp.zeros((rows, tile), F32)
                for _ in range(3):
                    high = chosen.astype(BF16)
                    chosen = chosen - high.astype(F32)
                    spread += transposed_dot(own, high)
                total[:, pl.ds(at, tile)] += spread

        if last:
            first = lax.axis_index("hid") * local if local < rows else 0
            outs[0][...] = total[pl.ds(pl.multiple_of(first, local), local), :]
            theirs = local - first if local < rows else 0
            outs[1][...] = total[pl.ds(pl.multiple_of(theirs, local), local), :].astype(BF16)
            sums = jnp.sum(total[...], axis=1, keepdims=True)
            outs[2][...] = jnp.broadcast_to(sums, (rows, 128)).T[0:1, :]

    if last:
        shapes = [((local, columns), F32), ((local, columns), BF16), ((1, rows), F32)]
    else:
        shapes = [((seats, tile), F32)]
    return pl.pallas_call(
        kernel,
        in_specs=[SMEM] + [VMEM] * len(arrays) + [VMEM, HBM, VMEM, VMEM] + [VMEM] * started,
        out_specs=[VMEM] * len(shapes),
        scratch_shapes=[
            pltpu.VMEM((count, BATCH, UNIT, width), BF16),
            pltpu.VMEM((count, BATCH * GROUP, width), BF16),
            pltpu.VMEM((rows, columns), F32),
            pltpu.SemaphoreType.DMA((count, BATCH)),
        ],
        out_shape=[jax.ShapeDtypeStruct(*shape) for shape in shapes],
        compiler_params=params(12),
        cost_estimate=cheap(),
        name="piece_scores",
    )(head, *arrays, select, look, emission, edges, *([before] if started else []))


def body(sizes, posterior, transition, emission, advance, dfa_state, edge_next, token_edge, allowed):
    vocab_size, hid_size = sizes
    rows = posterior.shape[0]
    hidden = transition.shape[1]
    slots = edge_next.shape[1]
    chips = vocab_size // 2
    width = hidden // vocab_size
    direct = chips == 8 and width % 128 == 0
    local = rows // hid_size
    first = lax.axis_index("hid") * local
    blocks = allowed.shape[1]
    tile = min(2, blocks) * BLK

    def swap(array, bits):
        return lax.ppermute(array, "vocab", [(i, i ^ bits) for i in range(vocab_size)])

    def made_ready(allowed, dfa_state, edge_next, token_edge, advance):
        return prepare(allowed.T, dfa_state[None, :], edge_next, token_edge, advance, tile)

    small = (allowed, dfa_state, edge_next, token_edge, advance)
    if direct:
        away = half_product(posterior, transition, True, ORDER, chips, width)
        came = swap(away, 1)
        kept = half_product(posterior, transition, False, ORDER, chips, width)
        parts = [(kept[n : n + 2].astype(F32) + came[n : n + 2].astype(F32)).astype(BF16) for n in (0, 2, 4, 6)]
        parts, small = lax.optimization_barrier((parts, small))
        far = swap(parts[0], 2)
        near = swap(parts[2], 2)
        far, small = lax.optimization_barrier((far, small))
        far = parts[1].astype(F32) + far.astype(F32)
        sent = [swap(far[0].astype(BF16), 8), swap(far[1].astype(BF16), 12)]
        near = parts[3].astype(F32) + near.astype(F32)
        sent.append(swap(near[1].astype(BF16), 4))
        head, select, edges, look = made_ready(*small)
        sent, head, select, edges, look = lax.optimization_barrier((sent, head, select, edges, look))
        own = near[0] + sent[0].astype(F32) + sent[1].astype(F32) + sent[2].astype(F32)
        own = own.astype(BF16)

        far = [swap(own, 8), swap(own, 12)]
        near = jnp.stack([own, swap(own, 4)])
        batches = [(near, NEAR_SAME)]
        batches.append((swap(near, 2), NEAR_OTHER))
        far = jnp.stack(far)
        batches.append((far, FAR_SAME))
        batches.append((swap(far, 2), FAR_OTHER))

        def one_batch(array, bits, before, last):
            def places():
                return [piece_place(chips, other, b) for other in (False, True) for b in bits]

            return piece_scores(
                [array, swap(array, 1)], places, head, select, look, emission, edges, before, slots, tile, last, local
            )

    else:
        own = lax.psum_scatter(
            jnp.dot(posterior, transition, preferred_element_type=F32), "vocab", scatter_dimension=0, tiled=True
        ).astype(BF16)
        prior = lax.all_gather(own, "vocab", axis=0, tiled=True)
        head, select, edges, look = made_ready(*small)
        wide = min(512, hidden)
        batches = [(prior[None, :, wide * j : wide * (j + 1)], j) for j in range(hidden // wide)]

        def one_batch(array, j, before, last):
            return piece_scores(
                [array], lambda: [j], head, select, look, emission, edges, before, slots, tile, last, rows
            )

    chosen = None
    for n, (array, where) in enumerate(batches):
        got = one_batch(array, where, chosen, n == len(batches) - 1)
        chosen = got[0]
    mine, theirs, part = got

    if hid_size == 2:
        part = part + lax.ppermute(part, "hid", [(0, 1), (1, 0)])
        bits = vocab_size // 2
        while bits:
            part = part + swap(part, bits)
            bits //= 2
        totals = lax.dynamic_slice_in_dim(part[0], first, local, 0)
        mine = mine + lax.ppermute(theirs, "hid", [(0, 1), (1, 0)]).astype(F32)
    else:
        mine = lax.psum_scatter(theirs, "hid", scatter_dimension=0, tiled=True).astype(F32)
        totals = lax.psum(jnp.sum(mine, axis=1), "vocab")
    mask = jnp.repeat(lax.dynamic_slice_in_dim(allowed, first, local, 0), BLK, axis=1) > 0
    safe = jnp.where(mask, mine, jnp.float32(1.0))
    return jnp.where(mask, jnp.log(safe) - jnp.log(totals)[:, None], jnp.float32(0.0))


def solution(mesh):
    in_specs = (
        P(None, "vocab"),
        P("vocab", "hid"),
        P("hid", "vocab"),
        P(None, "hid"),
        P(),
        P(),
        P(None, "vocab"),
        P(None, "vocab"),
    )
    sizes = (mesh.shape["vocab"], mesh.shape["hid"])
    return jax.shard_map(
        functools.partial(body, sizes), mesh=mesh, in_specs=in_specs, out_specs=P("hid", "vocab"), check_vma=False
    )
```

```python
import functools
import jax
import jax.numpy as jnp
from jax import lax
from jax.experimental import pallas as pl
from jax.experimental.pallas import tpu as pltpu
from jax.sharding import PartitionSpec as P

BLK = 128
GROUP = 32
UNIT = 256
BATCH = 4
CHEAP = 1 << 20
BF16 = jnp.bfloat16
F32 = jnp.float32
FAR_OTHER, FAR_SAME, NEAR_OTHER, NEAR_SAME = (5, 7), (4, 6), (1, 3), (0, 2)


def params(mib):
    return pltpu.CompilerParams(vmem_limit_bytes=mib << 20)


def cheap():
    return pl.CostEstimate(flops=CHEAP, bytes_accessed=CHEAP, transcendentals=0)


def piece_place(chips, other, bits):
    me = lax.axis_index("vocab")
    core, chip = lax.rem(me, 2), lax.div(me, 2)
    return (1 - core if other else core) * chips + (chip ^ bits)


def transposed_dot(a, b):
    return lax.dot_general(a, b, (((0,), (0,)), ((), ())), preferred_element_type=F32)


def in_hbm(array):
    return pltpu.with_memory_space_constraint(array, pltpu.HBM)


SMEM = pl.BlockSpec(memory_space=pltpu.SMEM)
VMEM = pl.BlockSpec(memory_space=pltpu.VMEM)
HBM = pl.BlockSpec(memory_space=pltpu.HBM)


def half_product(posterior, transition, other, order, chips, width):
    rows, depth = posterior.shape
    pieces = len(order)

    def kernel(post_ref, trans_ref, out_ref, held, arrived):
        def copy(n):
            first = piece_place(chips, other, order[n])
            columns = pl.ds(pl.multiple_of(first * width, width), width)
            return pltpu.make_async_copy(trans_ref.at[:, columns], held.at[n], arrived.at[n])

        for n in range(pieces):
            copy(n).start()
        for n in range(pieces):
            copy(n).wait()
            out_ref[n] = jnp.dot(post_ref[...], held[n], preferred_element_type=F32).astype(BF16)

    return pl.pallas_call(
        kernel,
        in_specs=[VMEM, HBM],
        out_specs=VMEM,
        out_shape=jax.ShapeDtypeStruct((pieces, rows, width), BF16),
        scratch_shapes=[
            pltpu.VMEM((pieces, depth, width), BF16),
            pltpu.SemaphoreType.DMA((pieces,)),
        ],
        compiler_params=params(24),
        cost_estimate=cheap(),
        name="prior_half",
    )(posterior, in_hbm(transition))


def take_seats(allowed, state, edge_next, token_edge, tile):
    blocks, rows = allowed.shape
    states, columns = token_edge.shape
    slots = edge_next.shape[1]
    tiles = columns // tile
    each = tile // BLK
    seats = tiles * rows

    def kernel(allow_ref, state_ref, next_ref, token_hbm, head_ref, select_ref, after_ref, edge_ref, token_ref, came):
        inward = pltpu.make_async_copy(token_hbm, token_ref, came)
        inward.start()
        who = (lax.broadcasted_iota(jnp.int32, (states, rows), 0) == state_ref[...]).astype(F32).astype(BF16)
        allow = allow_ref[...].astype(F32)
        earlier = lax.broadcasted_iota(jnp.int32, (rows, rows), 0) < lax.broadcasted_iota(jnp.int32, (rows, rows), 1)
        earlier = earlier.astype(F32).astype(BF16)
        number = lax.broadcasted_iota(jnp.int32, (seats, rows), 0)
        taken = jnp.zeros((seats, rows), F32)
        used = jnp.int32(0)
        for t in range(tiles):
            need = allow[t * each : t * each + 1]
            for b in range(1, each):
                need = jnp.maximum(need, allow[t * each + b : t * each + b + 1])
            rank = jnp.dot(jnp.broadcast_to(need, (8, rows)).astype(BF16), earlier, preferred_element_type=F32)[0:1]
            units = (jnp.sum(need).astype(jnp.int32) + GROUP - 1) // GROUP
            seat = jnp.where(need > 0, rank.astype(jnp.int32) + used * GROUP, -1)
            taken += (number == seat).astype(F32)

            @pl.loop(0, units)
            def _(u):
                head_ref[1 + used + u] = t

            used = used + units
        head_ref[0] = used
        taken = taken.astype(BF16)
        select_ref[...] = taken
        following = transposed_dot(who, next_ref[...].astype(F32).astype(BF16))
        after_ref[...] = jnp.dot(taken, following.astype(BF16), preferred_element_type=F32).astype(jnp.int32)
        allow = allow.astype(BF16)
        block = lax.broadcasted_iota(jnp.int32, (blocks, columns), 1) // BLK
        spread = (block == lax.broadcasted_iota(jnp.int32, (blocks, columns), 0)).astype(F32).astype(BF16)
        mask = transposed_dot(allow, spread)
        inward.wait()
        token = token_ref[...].astype(F32).astype(BF16)
        edge_ref[...] = jnp.where(mask > 0, transposed_dot(who, token), float(slots)).astype(BF16)

    return pl.pallas_call(
        kernel,
        in_specs=[VMEM] * 3 + [HBM],
        out_specs=[SMEM, VMEM, VMEM, VMEM],
        scratch_shapes=[pltpu.VMEM((states, columns), jnp.int32), pltpu.SemaphoreType.DMA],
        out_shape=[
            jax.ShapeDtypeStruct((1 + seats // GROUP,), jnp.int32),
            jax.ShapeDtypeStruct((seats, rows), BF16),
            jax.ShapeDtypeStruct((seats, slots), jnp.int32),
            jax.ShapeDtypeStruct((rows, columns), BF16),
        ],
        compiler_params=params(16),
        cost_estimate=cheap(),
        name="take_seats",
    )(allowed, state, edge_next, token_edge)


def successor_rows(head, after, advance):
    seats, slots = after.shape
    states, hidden = advance.shape
    width = min(1024, hidden)
    steps = hidden // width
    full = BATCH * UNIT

    def kernel(head_ref, after_ref, adv_hbm, first_ref, rest_ref, adv_ref, hot, held, left, came):
        def inward(n):
            span = pl.ds(n * width, width)
            return pltpu.make_async_copy(adv_hbm.at[:, span], adv_ref.at[:, span], came.at[n])

        for n in range(steps):
            inward(n).start()
        names = lax.broadcasted_iota(jnp.int32, (GROUP, states), 1)

        def mark(c):
            for u in range(BATCH):
                succ = after_ref[pl.ds(pl.multiple_of((c * BATCH + u) * GROUP, GROUP), GROUP), :]
                for k in range(slots):
                    hot[u * UNIT + k * GROUP : u * UNIT + (k + 1) * GROUP, :] = (
                        (names == succ[:, k : k + 1]).astype(F32).astype(BF16)
                    )

        def rows(n):
            span = slice(n * width, (n + 1) * width)
            return jnp.dot(hot[...], adv_ref[:, span], preferred_element_type=F32).astype(BF16)

        def copy(c, n):
            span = pl.ds(pl.multiple_of(c * full, full), full)
            return pltpu.make_async_copy(held, rest_ref.at[span, pl.ds(n * width, width)], left)

        mark(0)
        for n in range(steps):
            inward(n).wait()
            first_ref[:, n * width : (n + 1) * width] = rows(n)

        @pl.loop(1, (head_ref[0] + BATCH - 1) // BATCH)
        def _(c):
            mark(c)
            for n in range(steps):
                held[...] = rows(n)
                copy(c, n).start()
                copy(c, n).wait()

    return pl.pallas_call(
        kernel,
        in_specs=[SMEM, VMEM, HBM],
        out_specs=[VMEM, HBM],
        scratch_shapes=[
            pltpu.VMEM((states, hidden), BF16),
            pltpu.VMEM((full, states), BF16),
            pltpu.VMEM((full, width), BF16),
            pltpu.SemaphoreType.DMA,
            pltpu.SemaphoreType.DMA((steps,)),
        ],
        out_shape=[pltpu.VMEM((full, hidden), BF16), jax.ShapeDtypeStruct((seats * slots, hidden), BF16)],
        compiler_params=params(16),
        cost_estimate=cheap(),
        name="successor_rows",
    )(head, after, advance)


def stage(emission):
    deep = emission.shape[0] // 8

    def kernel(hbm, out_ref, came):
        copies = []
        for n in range(8):
            span = pl.ds(n * deep, deep)
            copies.append(pltpu.make_async_copy(hbm.at[span, :], out_ref.at[span, :], came.at[n]))
        for copy in copies:
            copy.start()
        for copy in copies:
            copy.wait()

    return pl.pallas_call(
        kernel,
        in_specs=[HBM],
        out_specs=VMEM,
        out_shape=pltpu.VMEM(emission.shape, BF16),
        scratch_shapes=[pltpu.SemaphoreType.DMA((8,))],
        compiler_params=params(16),
        cost_estimate=cheap(),
        name="stage",
    )(emission)


def piece_scores(arrays, places, head, select, look, emission, edges, before, slots, tile, last, local):
    each, rows, width = arrays[0].shape
    count = len(arrays) * each
    columns = emission.shape[1]
    seats = select.shape[0]
    started = before is not None

    def kernel(head_ref, *refs):
        piece_refs = refs[: len(arrays)]
        select_ref, near_ref, look_ref, emit_ref, edge_ref = refs[len(arrays) : len(arrays) + 5]
        before_ref = refs[len(arrays) + 5] if started else None
        looks, prior, total, arrived = refs[-4:]
        outs = refs[len(arrays) + 5 + started : -4]
        units = head_ref[0]
        deep = [pl.ds(pl.multiple_of(place * width, width), width) for place in places()]

        def look_copy(i, c, u):
            here = pl.ds(pl.multiple_of((c * BATCH + u) * UNIT, UNIT), UNIT)
            return pltpu.make_async_copy(look_ref.at[here, deep[i]], looks.at[i, u], arrived.at[i, u])

        if last:
            total[...] = jnp.zeros_like(total)

        def spread_prior(c):
            span = pl.ds(pl.multiple_of(c * BATCH * GROUP, BATCH * GROUP), BATCH * GROUP)
            for i in range(count):
                prior[i] = jnp.dot(
                    select_ref[span, :], piece_refs[i // each][i % each], preferred_element_type=F32
                ).astype(BF16)

        def one_unit(c, u, rows_of):
            at = pl.multiple_of(head_ref[1 + c * BATCH + u] * tile, tile)
            span = pl.ds(pl.multiple_of((c * BATCH + u) * GROUP, GROUP), GROUP)
            seat = pl.ds(pl.multiple_of(u * GROUP, GROUP), GROUP)
            values = None
            for i in range(count):
                rowed = rows_of(i, u).reshape(slots, GROUP, width)
                weighted = (rowed * prior[i, seat, :][None]).reshape(UNIT, width)
                part = jnp.dot(weighted, emit_ref[deep[i], pl.ds(at, tile)], preferred_element_type=F32)
                values = part if values is None else values + part
            own = select_ref[span, :]
            edge = jnp.dot(own, edge_ref[:, pl.ds(at, tile)], preferred_element_type=F32)
            chosen = before_ref[span, :] if started else jnp.zeros((GROUP, tile), F32)
            for k in range(slots):
                chosen += jnp.where(edge == k, values[k * GROUP : (k + 1) * GROUP], 0.0)
            if not last:
                outs[0][span, :] = chosen
                return
            spread = jnp.zeros((rows, tile), F32)
            for _ in range(3):
                high = chosen.astype(BF16)
                chosen = chosen - high.astype(F32)
                spread += transposed_dot(own, high)
            total[:, pl.ds(at, tile)] += spread

        spread_prior(0)

        @pl.loop(0, jnp.minimum(units, BATCH))
        def _(u):
            one_unit(0, u, lambda i, u: near_ref[pl.ds(pl.multiple_of(u * UNIT, UNIT), UNIT), deep[i]])

        @pl.loop(1, (units + BATCH - 1) // BATCH)
        def _(c):
            here = jnp.minimum(units - c * BATCH, BATCH)

            @pl.loop(0, here)
            def _(u):
                for i in range(count):
                    look_copy(i, c, u).start()

            spread_prior(c)

            @pl.loop(0, here)
            def _(u):
                for i in range(count):
                    look_copy(i, c, u).wait()
                one_unit(c, u, lambda i, u: looks[i, u])

        if last:
            first = lax.axis_index("hid") * local if local < rows else 0
            outs[0][...] = total[pl.ds(pl.multiple_of(first, local), local), :]
            theirs = local - first if local < rows else 0
            outs[1][...] = total[pl.ds(pl.multiple_of(theirs, local), local), :].astype(BF16)
            sums = jnp.sum(total[...], axis=1, keepdims=True)
            outs[2][...] = jnp.broadcast_to(sums, (rows, 128)).T[0:1, :]

    if last:
        shapes = [((local, columns), F32), ((local, columns), BF16), ((1, rows), F32)]
    else:
        shapes = [((seats, tile), F32)]
    return pl.pallas_call(
        kernel,
        in_specs=[SMEM] + [VMEM] * len(arrays) + [VMEM, VMEM, HBM, VMEM, VMEM] + [VMEM] * started,
        out_specs=[VMEM] * len(shapes),
        scratch_shapes=[
            pltpu.VMEM((count, BATCH, UNIT, width), BF16),
            pltpu.VMEM((count, BATCH * GROUP, width), BF16),
            pltpu.VMEM((rows, columns), F32),
            pltpu.SemaphoreType.DMA((count, BATCH)),
        ],
        out_shape=[jax.ShapeDtypeStruct(*shape) for shape in shapes],
        compiler_params=params(16),
        cost_estimate=cheap(),
        name="piece_scores",
    )(head, *arrays, select, *look, emission, edges, *([before] if started else []))


def body(sizes, posterior, transition, emission, advance, dfa_state, edge_next, token_edge, allowed):
    vocab_size, hid_size = sizes
    rows = posterior.shape[0]
    hidden = transition.shape[1]
    slots = edge_next.shape[1]
    chips = vocab_size // 2
    width = hidden // vocab_size
    direct = chips == 8 and width % 128 == 0
    local = rows // hid_size
    first = lax.axis_index("hid") * local
    blocks = allowed.shape[1]
    tile = min(2, blocks) * BLK

    def swap(array, bits):
        return lax.ppermute(array, "vocab", [(i, i ^ bits) for i in range(vocab_size)])

    def seated(allowed, dfa_state, edge_next, token_edge):
        return take_seats(allowed.T, dfa_state[None, :], edge_next, in_hbm(token_edge), tile)

    small = (allowed, dfa_state, edge_next, token_edge)
    if direct:
        order = FAR_OTHER + FAR_SAME + NEAR_OTHER + NEAR_SAME
        away = half_product(posterior, transition, True, order, chips, width)
        came = swap(away, 1)
        kept = half_product(posterior, transition, False, order, chips, width)
        parts = [(kept[n : n + 2].astype(F32) + came[n : n + 2].astype(F32)).astype(BF16) for n in (0, 2, 4, 6)]
        far = swap(parts[0], 2)
        parts, small = lax.optimization_barrier((parts, small))
        near = swap(parts[2], 2)
        head, select, after, edges = seated(*small)
        far, head, select, after, edges = lax.optimization_barrier((far, head, select, after, edges))
        far = parts[1].astype(F32) + far.astype(F32)
        sent = [swap(far[0].astype(BF16), 8), swap(far[1].astype(BF16), 12)]
        near = parts[3].astype(F32) + near.astype(F32)
        sent.append(swap(near[1].astype(BF16), 4))
        look = successor_rows(head, after, in_hbm(advance))
        sent, look = lax.optimization_barrier((sent, look))
        own = near[0] + sent[0].astype(F32) + sent[1].astype(F32) + sent[2].astype(F32)
        own = own.astype(BF16)

        own, emission = lax.optimization_barrier((own, emission))
        far = [swap(own, 8), swap(own, 12)]
        far, emission = lax.optimization_barrier((far, stage(in_hbm(emission))))
        far = jnp.stack(far)
        near = jnp.stack([own, swap(own, 2)])
        batches = [((near, far), (0, 1, 4, 6)), ((swap(near, 4), swap(far, 2)), (2, 3, 5, 7))]

        def one_batch(arrays, bits, before, last):
            def places():
                groups = (bits[:2], bits[2:])
                return [piece_place(chips, other, b) for group in groups for other in (False, True) for b in group]

            first, second = arrays
            if before is not None:
                first, second, before = lax.optimization_barrier((first, second, before))
            arrays = [first, swap(first, 1), second, swap(second, 1)]
            return piece_scores(
                arrays, places, head, select, look, emission, edges, before, slots, tile, last, local
            )

    else:
        own = lax.psum_scatter(
            jnp.dot(posterior, transition, preferred_element_type=F32), "vocab", scatter_dimension=0, tiled=True
        ).astype(BF16)
        prior = lax.all_gather(own, "vocab", axis=0, tiled=True)
        head, select, after, edges = seated(*small)
        look = successor_rows(head, after, in_hbm(advance))
        wide = min(512, hidden)
        batches = [(prior[None, :, wide * j : wide * (j + 1)], j) for j in range(hidden // wide)]

        def one_batch(array, j, before, last):
            return piece_scores(
                [array], lambda: [j], head, select, look, emission, edges, before, slots, tile, last, rows
            )

    chosen = None
    for n, (array, where) in enumerate(batches):
        got = one_batch(array, where, chosen, n == len(batches) - 1)
        chosen = got[0]
    mine, theirs, part = got

    if hid_size == 2:
        bits = vocab_size // 2
        while bits:
            part = part + swap(part, bits)
            if bits == vocab_size // 2:
                part, theirs = lax.optimization_barrier((part, theirs))
                theirs = lax.ppermute(theirs, "hid", [(0, 1), (1, 0)])
            bits //= 2
        part, theirs = lax.optimization_barrier((part, theirs))
        part = part + lax.ppermute(part, "hid", [(0, 1), (1, 0)])
        totals = lax.dynamic_slice_in_dim(part[0], first, local, 0)
        mine = mine + theirs.astype(F32)
    else:
        mine = lax.psum_scatter(theirs, "hid", scatter_dimension=0, tiled=True).astype(F32)
        totals = lax.psum(jnp.sum(mine, axis=1), "vocab")
    mask = jnp.repeat(lax.dynamic_slice_in_dim(allowed, first, local, 0), BLK, axis=1) > 0
    safe = jnp.where(mask, mine, jnp.float32(1.0))
    return jnp.where(mask, jnp.log(safe) - jnp.log(totals)[:, None], jnp.float32(0.0))


def solution(mesh):
    in_specs = (
        P(None, "vocab"),
        P("vocab", "hid"),
        P("hid", "vocab"),
        P(None, "hid"),
        P(),
        P(),
        P(None, "vocab"),
        P(None, "vocab"),
    )
    sizes = (mesh.shape["vocab"], mesh.shape["hid"])
    return jax.shard_map(
        functools.partial(body, sizes), mesh=mesh, in_specs=in_specs, out_specs=P("hid", "vocab"), check_vma=False
    )
```

```python
import functools
import jax
import jax.numpy as jnp
from jax import lax
from jax.experimental import pallas as pl
from jax.experimental.pallas import tpu as pltpu
from jax.sharding import PartitionSpec as P

BLK = 128
GROUP = 32
UNIT = 256
BATCH = 4
CHEAP = 1 << 20
BF16 = jnp.bfloat16
F32 = jnp.float32
FAR_OTHER, FAR_SAME, NEAR_OTHER, NEAR_SAME = (5, 7), (4, 6), (1, 3), (0, 2)


def params(mib):
    return pltpu.CompilerParams(vmem_limit_bytes=mib << 20)


def cheap():
    return pl.CostEstimate(flops=CHEAP, bytes_accessed=CHEAP, transcendentals=0)


def piece_place(chips, other, bits):
    me = lax.axis_index("vocab")
    core, chip = lax.rem(me, 2), lax.div(me, 2)
    return (1 - core if other else core) * chips + (chip ^ bits)


def transposed_dot(a, b):
    return lax.dot_general(a, b, (((0,), (0,)), ((), ())), preferred_element_type=F32)


def in_hbm(array):
    return pltpu.with_memory_space_constraint(array, pltpu.HBM)


SMEM = pl.BlockSpec(memory_space=pltpu.SMEM)
VMEM = pl.BlockSpec(memory_space=pltpu.VMEM)
HBM = pl.BlockSpec(memory_space=pltpu.HBM)


def half_product(posterior, transition, other, order, chips, width):
    rows, depth = posterior.shape
    pieces = len(order)

    def kernel(post_ref, trans_ref, out_ref, held, arrived):
        def copy(n):
            first = piece_place(chips, other, order[n])
            columns = pl.ds(pl.multiple_of(first * width, width), width)
            return pltpu.make_async_copy(trans_ref.at[:, columns], held.at[n], arrived.at[n])

        for n in range(pieces):
            copy(n).start()
        for n in range(pieces):
            copy(n).wait()
            out_ref[n] = jnp.dot(post_ref[...], held[n], preferred_element_type=F32).astype(BF16)

    return pl.pallas_call(
        kernel,
        in_specs=[VMEM, HBM],
        out_specs=VMEM,
        out_shape=jax.ShapeDtypeStruct((pieces, rows, width), BF16),
        scratch_shapes=[
            pltpu.VMEM((pieces, depth, width), BF16),
            pltpu.SemaphoreType.DMA((pieces,)),
        ],
        compiler_params=params(24),
        cost_estimate=cheap(),
        name="prior_half",
    )(posterior, in_hbm(transition))


def take_seats(allowed, state, edge_next, token_edge, tile):
    blocks, rows = allowed.shape
    states, columns = token_edge.shape
    slots = edge_next.shape[1]
    tiles = columns // tile
    each = tile // BLK
    seats = tiles * rows

    def kernel(allow_ref, state_ref, next_ref, token_hbm, head_ref, select_ref, after_ref, edge_ref, token_ref, came):
        inward = pltpu.make_async_copy(token_hbm, token_ref, came)
        inward.start()
        who = (lax.broadcasted_iota(jnp.int32, (states, rows), 0) == state_ref[...]).astype(F32).astype(BF16)
        allow = allow_ref[...].astype(F32)
        earlier = lax.broadcasted_iota(jnp.int32, (rows, rows), 0) < lax.broadcasted_iota(jnp.int32, (rows, rows), 1)
        earlier = earlier.astype(F32).astype(BF16)
        number = lax.broadcasted_iota(jnp.int32, (seats, rows), 0)
        taken = jnp.zeros((seats, rows), F32)
        used = jnp.int32(0)
        for t in range(tiles):
            need = allow[t * each : t * each + 1]
            for b in range(1, each):
                need = jnp.maximum(need, allow[t * each + b : t * each + b + 1])
            rank = jnp.dot(jnp.broadcast_to(need, (8, rows)).astype(BF16), earlier, preferred_element_type=F32)[0:1]
            units = (jnp.sum(need).astype(jnp.int32) + GROUP - 1) // GROUP
            seat = jnp.where(need > 0, rank.astype(jnp.int32) + used * GROUP, -1)
            taken += (number == seat).astype(F32)

            @pl.loop(0, units)
            def _(u):
                head_ref[1 + used + u] = t

            used = used + units
        head_ref[0] = used
        taken = taken.astype(BF16)
        select_ref[...] = taken
        following = transposed_dot(who, next_ref[...].astype(F32).astype(BF16))
        after_ref[...] = jnp.dot(taken, following.astype(BF16), preferred_element_type=F32).astype(jnp.int32)
        allow = allow.astype(BF16)
        block = lax.broadcasted_iota(jnp.int32, (blocks, columns), 1) // BLK
        spread = (block == lax.broadcasted_iota(jnp.int32, (blocks, columns), 0)).astype(F32).astype(BF16)
        mask = transposed_dot(allow, spread)
        inward.wait()
        token = token_ref[...].astype(F32).astype(BF16)
        edge_ref[...] = jnp.where(mask > 0, transposed_dot(who, token), float(slots)).astype(BF16)

    return pl.pallas_call(
        kernel,
        in_specs=[VMEM] * 3 + [HBM],
        out_specs=[SMEM, VMEM, VMEM, VMEM],
        scratch_shapes=[pltpu.VMEM((states, columns), jnp.int32), pltpu.SemaphoreType.DMA],
        out_shape=[
            jax.ShapeDtypeStruct((1 + seats // GROUP,), jnp.int32),
            jax.ShapeDtypeStruct((seats, rows), BF16),
            jax.ShapeDtypeStruct((seats, slots), jnp.int32),
            jax.ShapeDtypeStruct((rows, columns), BF16),
        ],
        compiler_params=params(16),
        cost_estimate=cheap(),
        name="take_seats",
    )(allowed, state, edge_next, token_edge)


def successor_rows(head, after, advance):
    seats, slots = after.shape
    states, hidden = advance.shape
    width = min(1024, hidden)
    steps = hidden // width
    full = BATCH * UNIT

    def kernel(head_ref, after_ref, adv_hbm, first_ref, rest_ref, adv_ref, hot, held, left, came):
        def inward(n):
            span = pl.ds(n * width, width)
            return pltpu.make_async_copy(adv_hbm.at[:, span], adv_ref.at[:, span], came.at[n])

        for n in range(steps):
            inward(n).start()
        names = lax.broadcasted_iota(jnp.int32, (GROUP, states), 1)

        def mark(c):
            for u in range(BATCH):
                succ = after_ref[pl.ds(pl.multiple_of((c * BATCH + u) * GROUP, GROUP), GROUP), :]
                for k in range(slots):
                    hot[u * UNIT + k * GROUP : u * UNIT + (k + 1) * GROUP, :] = (
                        (names == succ[:, k : k + 1]).astype(F32).astype(BF16)
                    )

        def rows(n):
            span = slice(n * width, (n + 1) * width)
            return jnp.dot(hot[...], adv_ref[:, span], preferred_element_type=F32).astype(BF16)

        def copy(c, n):
            span = pl.ds(pl.multiple_of(c * full, full), full)
            return pltpu.make_async_copy(held, rest_ref.at[span, pl.ds(n * width, width)], left)

        mark(0)
        for n in range(steps):
            inward(n).wait()
            first_ref[:, n * width : (n + 1) * width] = rows(n)

        @pl.loop(1, (head_ref[0] + BATCH - 1) // BATCH)
        def _(c):
            mark(c)
            for n in range(steps):
                held[...] = rows(n)
                copy(c, n).start()
                copy(c, n).wait()

    return pl.pallas_call(
        kernel,
        in_specs=[SMEM, VMEM, HBM],
        out_specs=[VMEM, HBM],
        scratch_shapes=[
            pltpu.VMEM((states, hidden), BF16),
            pltpu.VMEM((full, states), BF16),
            pltpu.VMEM((full, width), BF16),
            pltpu.SemaphoreType.DMA,
            pltpu.SemaphoreType.DMA((steps,)),
        ],
        out_shape=[pltpu.VMEM((full, hidden), BF16), jax.ShapeDtypeStruct((seats * slots, hidden), BF16)],
        compiler_params=params(16),
        cost_estimate=cheap(),
        name="successor_rows",
    )(head, after, advance)


def stage(emission):
    deep = emission.shape[0] // 8

    def kernel(hbm, out_ref, came):
        copies = []
        for n in range(8):
            span = pl.ds(n * deep, deep)
            copies.append(pltpu.make_async_copy(hbm.at[span, :], out_ref.at[span, :], came.at[n]))
        for copy in copies:
            copy.start()
        for copy in copies:
            copy.wait()

    return pl.pallas_call(
        kernel,
        in_specs=[HBM],
        out_specs=VMEM,
        out_shape=pltpu.VMEM(emission.shape, BF16),
        scratch_shapes=[pltpu.SemaphoreType.DMA((8,))],
        compiler_params=params(16),
        cost_estimate=cheap(),
        name="stage",
    )(emission)


def piece_scores(arrays, places, head, select, look, emission, edges, before, slots, tile, last, local):
    each, rows, width = arrays[0].shape
    count = len(arrays) * each
    columns = emission.shape[1]
    seats = select.shape[0]
    started = before is not None

    def kernel(head_ref, *refs):
        piece_refs = refs[: len(arrays)]
        select_ref, near_ref, look_ref, emit_ref, edge_ref = refs[len(arrays) : len(arrays) + 5]
        before_ref = refs[len(arrays) + 5] if started else None
        looks, prior, total, arrived = refs[-4:]
        outs = refs[len(arrays) + 5 + started : -4]
        units = head_ref[0]
        deep = [pl.ds(pl.multiple_of(place * width, width), width) for place in places()]

        def look_copy(i, c, u):
            here = pl.ds(pl.multiple_of((c * BATCH + u) * UNIT, UNIT), UNIT)
            return pltpu.make_async_copy(look_ref.at[here, deep[i]], looks.at[i, u], arrived.at[i, u])

        if last:
            total[...] = jnp.zeros_like(total)

        def spread_prior(c):
            span = pl.ds(pl.multiple_of(c * BATCH * GROUP, BATCH * GROUP), BATCH * GROUP)
            for i in range(count):
                prior[i] = jnp.dot(
                    select_ref[span, :], piece_refs[i // each][i % each], preferred_element_type=F32
                ).astype(BF16)

        def one_unit(c, u, rows_of):
            at = pl.multiple_of(head_ref[1 + c * BATCH + u] * tile, tile)
            span = pl.ds(pl.multiple_of((c * BATCH + u) * GROUP, GROUP), GROUP)
            seat = pl.ds(pl.multiple_of(u * GROUP, GROUP), GROUP)
            values = None
            for i in range(count):
                rowed = rows_of(i, u).reshape(slots, GROUP, width)
                weighted = (rowed * prior[i, seat, :][None]).reshape(UNIT, width)
                part = jnp.dot(weighted, emit_ref[deep[i], pl.ds(at, tile)], preferred_element_type=F32)
                values = part if values is None else values + part
            own = select_ref[span, :]
            edge = jnp.dot(own, edge_ref[:, pl.ds(at, tile)], preferred_element_type=F32)
            chosen = before_ref[span, :] if started else jnp.zeros((GROUP, tile), F32)
            for k in range(slots):
                chosen += jnp.where(edge == k, values[k * GROUP : (k + 1) * GROUP], 0.0)
            if not last:
                outs[0][span, :] = chosen
                return
            spread = jnp.zeros((rows, tile), F32)
            for _ in range(3):
                high = chosen.astype(BF16)
                chosen = chosen - high.astype(F32)
                spread += transposed_dot(own, high)
            total[:, pl.ds(at, tile)] += spread

        spread_prior(0)

        @pl.loop(0, jnp.minimum(units, BATCH))
        def _(u):
            one_unit(0, u, lambda i, u: near_ref[pl.ds(pl.multiple_of(u * UNIT, UNIT), UNIT), deep[i]])

        @pl.loop(1, (units + BATCH - 1) // BATCH)
        def _(c):
            here = jnp.minimum(units - c * BATCH, BATCH)

            @pl.loop(0, here)
            def _(u):
                for i in range(count):
                    look_copy(i, c, u).start()

            spread_prior(c)

            @pl.loop(0, here)
            def _(u):
                for i in range(count):
                    look_copy(i, c, u).wait()
                one_unit(c, u, lambda i, u: looks[i, u])

        if last:
            first = lax.axis_index("hid") * local if local < rows else 0
            outs[0][...] = total[pl.ds(pl.multiple_of(first, local), local), :]
            theirs = local - first if local < rows else 0
            outs[1][...] = total[pl.ds(pl.multiple_of(theirs, local), local), :].astype(BF16)
            sums = jnp.sum(total[...], axis=1, keepdims=True)
            outs[2][...] = jnp.broadcast_to(sums, (rows, 128)).T[0:1, :]

    if last:
        shapes = [((local, columns), F32), ((local, columns), BF16), ((1, rows), F32)]
    else:
        shapes = [((seats, tile), F32)]
    return pl.pallas_call(
        kernel,
        in_specs=[SMEM] + [VMEM] * len(arrays) + [VMEM, VMEM, HBM, VMEM, VMEM] + [VMEM] * started,
        out_specs=[VMEM] * len(shapes),
        scratch_shapes=[
            pltpu.VMEM((count, BATCH, UNIT, width), BF16),
            pltpu.VMEM((count, BATCH * GROUP, width), BF16),
            pltpu.VMEM((rows, columns), F32),
            pltpu.SemaphoreType.DMA((count, BATCH)),
        ],
        out_shape=[jax.ShapeDtypeStruct(*shape) for shape in shapes],
        compiler_params=params(16),
        cost_estimate=cheap(),
        name="piece_scores",
    )(head, *arrays, select, *look, emission, edges, *([before] if started else []))


def body(sizes, posterior, transition, emission, advance, dfa_state, edge_next, token_edge, allowed):
    vocab_size, hid_size = sizes
    rows = posterior.shape[0]
    hidden = transition.shape[1]
    slots = edge_next.shape[1]
    chips = vocab_size // 2
    width = hidden // vocab_size
    direct = chips == 8 and width % 128 == 0
    local = rows // hid_size
    first = lax.axis_index("hid") * local
    blocks = allowed.shape[1]
    tile = min(2, blocks) * BLK

    def swap(array, bits):
        return lax.ppermute(array, "vocab", [(i, i ^ bits) for i in range(vocab_size)])

    def seated(allowed, dfa_state, edge_next, token_edge):
        return take_seats(allowed.T, dfa_state[None, :], edge_next, in_hbm(token_edge), tile)

    small = (allowed, dfa_state, edge_next, token_edge)
    if direct:
        order = FAR_OTHER + FAR_SAME + NEAR_OTHER + NEAR_SAME
        away = half_product(posterior, transition, True, order, chips, width)
        came = swap(away, 1)
        kept = half_product(posterior, transition, False, order[:4], chips, width)
        parts = [(kept[n : n + 2].astype(F32) + came[n : n + 2].astype(F32)).astype(BF16) for n in (0, 2)]
        parts, posterior = lax.optimization_barrier((parts, posterior))
        far = swap(parts[0], 2)
        kept = half_product(posterior, transition, False, order[4:], chips, width)
        parts += [(kept[n : n + 2].astype(F32) + came[n + 4 : n + 6].astype(F32)).astype(BF16) for n in (0, 2)]
        parts, small = lax.optimization_barrier((parts, small))
        near = swap(parts[2], 2)
        head, select, after, edges = seated(*small)
        far, head, select, after, edges = lax.optimization_barrier((far, head, select, after, edges))
        far = parts[1].astype(F32) + far.astype(F32)
        sent = [swap(far[0].astype(BF16), 8), swap(far[1].astype(BF16), 12)]
        near = parts[3].astype(F32) + near.astype(F32)
        sent.append(swap(near[1].astype(BF16), 4))
        look = successor_rows(head, after, in_hbm(advance))
        sent, look = lax.optimization_barrier((sent, look))
        own = near[0] + sent[0].astype(F32) + sent[1].astype(F32) + sent[2].astype(F32)
        own = own.astype(BF16)

        own, emission = lax.optimization_barrier((own, emission))
        far = [swap(own, 8), swap(own, 12)]
        far, emission = lax.optimization_barrier((far, stage(in_hbm(emission))))
        far = jnp.stack(far)
        near = jnp.stack([own, swap(own, 2)])
        batches = [((near, far), (0, 1, 4, 6)), ((swap(near, 4), swap(far, 2)), (2, 3, 5, 7))]

        def one_batch(arrays, bits, before, last):
            def places():
                groups = (bits[:2], bits[2:])
                return [piece_place(chips, other, b) for group in groups for other in (False, True) for b in group]

            first, second = arrays
            if before is not None:
                first, second, before = lax.optimization_barrier((first, second, before))
            arrays = [first, swap(first, 1), second, swap(second, 1)]
            return piece_scores(
                arrays, places, head, select, look, emission, edges, before, slots, tile, last, local
            )

    else:
        own = lax.psum_scatter(
            jnp.dot(posterior, transition, preferred_element_type=F32), "vocab", scatter_dimension=0, tiled=True
        ).astype(BF16)
        prior = lax.all_gather(own, "vocab", axis=0, tiled=True)
        head, select, after, edges = seated(*small)
        look = successor_rows(head, after, in_hbm(advance))
        wide = min(512, hidden)
        batches = [(prior[None, :, wide * j : wide * (j + 1)], j) for j in range(hidden // wide)]

        def one_batch(array, j, before, last):
            return piece_scores(
                [array], lambda: [j], head, select, look, emission, edges, before, slots, tile, last, rows
            )

    chosen = None
    for n, (array, where) in enumerate(batches):
        got = one_batch(array, where, chosen, n == len(batches) - 1)
        chosen = got[0]
    mine, theirs, part = got

    if hid_size == 2:
        theirs = lax.ppermute(theirs, "hid", [(0, 1), (1, 0)])
        if direct:
            part = part + swap(part, 8) + swap(part, 12) + swap(part, 4)
            part = part + swap(part, 1)
            part, theirs = lax.optimization_barrier((part, theirs))
            across = [(i, i ^ 5) for i in range(2 * vocab_size)]
            beside = lax.ppermute(part, "hid", [(0, 1), (1, 0)])
            part = part + swap(part, 2) + beside + lax.ppermute(part, ("vocab", "hid"), across)
        else:
            part = lax.psum(part, ("vocab", "hid"))
        totals = lax.dynamic_slice_in_dim(part[0], first, local, 0)
        mine = mine + theirs.astype(F32)
    else:
        mine = lax.psum_scatter(theirs, "hid", scatter_dimension=0, tiled=True).astype(F32)
        totals = lax.psum(jnp.sum(mine, axis=1), "vocab")
    mask = jnp.repeat(lax.dynamic_slice_in_dim(allowed, first, local, 0), BLK, axis=1) > 0
    safe = jnp.where(mask, mine, jnp.float32(1.0))
    return jnp.where(mask, jnp.log(safe) - jnp.log(totals)[:, None], jnp.float32(0.0))


def solution(mesh):
    in_specs = (
        P(None, "vocab"),
        P("vocab", "hid"),
        P("hid", "vocab"),
        P(None, "hid"),
        P(),
        P(),
        P(None, "vocab"),
        P(None, "vocab"),
    )
    sizes = (mesh.shape["vocab"], mesh.shape["hid"])
    return jax.shard_map(
        functools.partial(body, sizes), mesh=mesh, in_specs=in_specs, out_specs=P("hid", "vocab"), check_vma=False
    )
```

```python
import functools
import jax
import jax.numpy as jnp
from jax import lax
from jax.experimental import pallas as pl
from jax.experimental.pallas import tpu as pltpu
from jax.sharding import PartitionSpec as P

BLK = 128
GROUP = 32
UNIT = 256
BATCH = 4
CHEAP = 1 << 20
BF16 = jnp.bfloat16
F32 = jnp.float32
FAR_OTHER, FAR_SAME, NEAR_OTHER, NEAR_SAME = (5, 7), (4, 6), (1, 3), (0, 2)


def params(mib):
    return pltpu.CompilerParams(vmem_limit_bytes=mib << 20)


def cheap():
    return pl.CostEstimate(flops=CHEAP, bytes_accessed=CHEAP, transcendentals=0)


def piece_place(chips, other, bits):
    me = lax.axis_index("vocab")
    core, chip = lax.rem(me, 2), lax.div(me, 2)
    return (1 - core if other else core) * chips + (chip ^ bits)


def transposed_dot(a, b):
    return lax.dot_general(a, b, (((0,), (0,)), ((), ())), preferred_element_type=F32)


def in_hbm(array):
    return pltpu.with_memory_space_constraint(array, pltpu.HBM)


SMEM = pl.BlockSpec(memory_space=pltpu.SMEM)
VMEM = pl.BlockSpec(memory_space=pltpu.VMEM)
HBM = pl.BlockSpec(memory_space=pltpu.HBM)


def half_product(posterior, transition, other, order, chips, width):
    rows, depth = posterior.shape
    pieces = len(order)

    def kernel(post_ref, trans_ref, out_ref, held, arrived):
        def copy(n):
            first = piece_place(chips, other, order[n])
            columns = pl.ds(pl.multiple_of(first * width, width), width)
            return pltpu.make_async_copy(trans_ref.at[:, columns], held.at[n], arrived.at[n])

        for n in range(pieces):
            copy(n).start()
        for n in range(pieces):
            copy(n).wait()
            out_ref[n] = jnp.dot(post_ref[...], held[n], preferred_element_type=F32).astype(BF16)

    return pl.pallas_call(
        kernel,
        in_specs=[VMEM, HBM],
        out_specs=VMEM,
        out_shape=jax.ShapeDtypeStruct((pieces, rows, width), BF16),
        scratch_shapes=[
            pltpu.VMEM((pieces, depth, width), BF16),
            pltpu.SemaphoreType.DMA((pieces,)),
        ],
        compiler_params=params(24),
        cost_estimate=cheap(),
        name="prior_half",
    )(posterior, in_hbm(transition))


def take_seats(allowed, state, edge_next, token_edge, tile):
    blocks, rows = allowed.shape
    states, columns = token_edge.shape
    slots = edge_next.shape[1]
    tiles = columns // tile
    each = tile // BLK
    seats = tiles * rows

    def kernel(allow_ref, state_ref, next_ref, token_hbm, head_ref, select_ref, after_ref, edge_ref, token_ref, came):
        inward = pltpu.make_async_copy(token_hbm, token_ref, came)
        inward.start()
        who = (lax.broadcasted_iota(jnp.int32, (states, rows), 0) == state_ref[...]).astype(F32).astype(BF16)
        allow = allow_ref[...].astype(F32)
        earlier = lax.broadcasted_iota(jnp.int32, (rows, rows), 0) < lax.broadcasted_iota(jnp.int32, (rows, rows), 1)
        earlier = earlier.astype(F32).astype(BF16)
        number = lax.broadcasted_iota(jnp.int32, (seats, rows), 0)
        taken = jnp.zeros((seats, rows), F32)
        used = jnp.int32(0)
        for t in range(tiles):
            need = allow[t * each : t * each + 1]
            for b in range(1, each):
                need = jnp.maximum(need, allow[t * each + b : t * each + b + 1])
            rank = jnp.dot(jnp.broadcast_to(need, (8, rows)).astype(BF16), earlier, preferred_element_type=F32)[0:1]
            units = (jnp.sum(need).astype(jnp.int32) + GROUP - 1) // GROUP
            seat = jnp.where(need > 0, rank.astype(jnp.int32) + used * GROUP, -1)
            taken += (number == seat).astype(F32)

            @pl.loop(0, units)
            def _(u):
                head_ref[1 + used + u] = t

            used = used + units
        head_ref[0] = used
        taken = taken.astype(BF16)
        select_ref[...] = taken
        following = transposed_dot(who, next_ref[...].astype(F32).astype(BF16))
        after_ref[...] = jnp.dot(taken, following.astype(BF16), preferred_element_type=F32).astype(jnp.int32)
        allow = allow.astype(BF16)
        block = lax.broadcasted_iota(jnp.int32, (blocks, columns), 1) // BLK
        spread = (block == lax.broadcasted_iota(jnp.int32, (blocks, columns), 0)).astype(F32).astype(BF16)
        mask = transposed_dot(allow, spread)
        inward.wait()
        token = token_ref[...].astype(F32).astype(BF16)
        edge_ref[...] = jnp.where(mask > 0, transposed_dot(who, token), float(slots)).astype(BF16)

    return pl.pallas_call(
        kernel,
        in_specs=[VMEM] * 3 + [HBM],
        out_specs=[SMEM, VMEM, VMEM, VMEM],
        scratch_shapes=[pltpu.VMEM((states, columns), jnp.int32), pltpu.SemaphoreType.DMA],
        out_shape=[
            jax.ShapeDtypeStruct((1 + seats // GROUP,), jnp.int32),
            jax.ShapeDtypeStruct((seats, rows), BF16),
            jax.ShapeDtypeStruct((seats, slots), jnp.int32),
            jax.ShapeDtypeStruct((rows, columns), BF16),
        ],
        compiler_params=params(12),
        cost_estimate=cheap(),
        name="take_seats",
    )(allowed, state, edge_next, token_edge)


def successor_rows(head, after, advance, emission):
    seats, slots = after.shape
    states, hidden = advance.shape
    width = min(1024, hidden)
    steps = hidden // width
    full = BATCH * UNIT
    deep = emission.shape[0] // 8

    def kernel(
        head_ref, after_ref, adv_hbm, emit_hbm, first_ref, rest_ref, emit_ref, adv_ref, hot, held, left, came, staged
    ):
        def stage(n):
            span = pl.ds(n * deep, deep)
            return pltpu.make_async_copy(emit_hbm.at[span, :], emit_ref.at[span, :], staged.at[n])

        def inward(n):
            span = pl.ds(n * width, width)
            return pltpu.make_async_copy(adv_hbm.at[:, span], adv_ref.at[:, span], came.at[n])

        for n in range(steps):
            inward(n).start()
        for n in range(8):
            stage(n).start()
        names = lax.broadcasted_iota(jnp.int32, (GROUP, states), 1)

        def mark(c):
            for u in range(BATCH):
                succ = after_ref[pl.ds(pl.multiple_of((c * BATCH + u) * GROUP, GROUP), GROUP), :]
                for k in range(slots):
                    hot[u * UNIT + k * GROUP : u * UNIT + (k + 1) * GROUP, :] = (
                        (names == succ[:, k : k + 1]).astype(F32).astype(BF16)
                    )

        def rows(n):
            span = slice(n * width, (n + 1) * width)
            return jnp.dot(hot[...], adv_ref[:, span], preferred_element_type=F32).astype(BF16)

        def copy(c, n):
            span = pl.ds(pl.multiple_of(c * full, full), full)
            return pltpu.make_async_copy(held, rest_ref.at[span, pl.ds(n * width, width)], left)

        mark(0)
        for n in range(steps):
            inward(n).wait()
            first_ref[:, n * width : (n + 1) * width] = rows(n)

        @pl.loop(1, (head_ref[0] + BATCH - 1) // BATCH)
        def _(c):
            mark(c)
            for n in range(steps):
                held[...] = rows(n)
                copy(c, n).start()
                copy(c, n).wait()

        for n in range(8):
            stage(n).wait()

    return pl.pallas_call(
        kernel,
        in_specs=[SMEM, VMEM, HBM, HBM],
        out_specs=[VMEM, HBM, VMEM],
        scratch_shapes=[
            pltpu.VMEM((states, hidden), BF16),
            pltpu.VMEM((full, states), BF16),
            pltpu.VMEM((full, width), BF16),
            pltpu.SemaphoreType.DMA,
            pltpu.SemaphoreType.DMA((steps,)),
            pltpu.SemaphoreType.DMA((8,)),
        ],
        out_shape=[
            pltpu.VMEM((full, hidden), BF16),
            jax.ShapeDtypeStruct((seats * slots, hidden), BF16),
            pltpu.VMEM(emission.shape, BF16),
        ],
        compiler_params=params(12),
        cost_estimate=cheap(),
        name="successor_rows",
    )(head, after, advance, emission)


def piece_scores(arrays, places, head, select, look, emission, edges, before, slots, tile, last, local):
    each, rows, width = arrays[0].shape
    count = len(arrays) * each
    columns = emission.shape[1]
    seats = select.shape[0]
    started = before is not None

    def kernel(head_ref, *refs):
        piece_refs = refs[: len(arrays)]
        select_ref, near_ref, look_ref, emit_ref, edge_ref = refs[len(arrays) : len(arrays) + 5]
        before_ref = refs[len(arrays) + 5] if started else None
        looks, prior, total, arrived = refs[-4:]
        outs = refs[len(arrays) + 5 + started : -4]
        units = head_ref[0]
        deep = [pl.ds(pl.multiple_of(place * width, width), width) for place in places()]

        def look_copy(i, c, u):
            here = pl.ds(pl.multiple_of((c * BATCH + u) * UNIT, UNIT), UNIT)
            return pltpu.make_async_copy(look_ref.at[here, deep[i]], looks.at[i, u], arrived.at[i, u])

        if last:
            total[...] = jnp.zeros_like(total)

        def spread_prior(c):
            span = pl.ds(pl.multiple_of(c * BATCH * GROUP, BATCH * GROUP), BATCH * GROUP)
            for i in range(count):
                prior[i] = jnp.dot(
                    select_ref[span, :], piece_refs[i // each][i % each], preferred_element_type=F32
                ).astype(BF16)

        def one_unit(c, u, rows_of):
            at = pl.multiple_of(head_ref[1 + c * BATCH + u] * tile, tile)
            span = pl.ds(pl.multiple_of((c * BATCH + u) * GROUP, GROUP), GROUP)
            seat = pl.ds(pl.multiple_of(u * GROUP, GROUP), GROUP)
            values = None
            for i in range(count):
                rowed = rows_of(i, u).reshape(slots, GROUP, width)
                weighted = (rowed * prior[i, seat, :][None]).reshape(UNIT, width)
                part = jnp.dot(weighted, emit_ref[deep[i], pl.ds(at, tile)], preferred_element_type=F32)
                values = part if values is None else values + part
            own = select_ref[span, :]
            edge = jnp.dot(own, edge_ref[:, pl.ds(at, tile)], preferred_element_type=F32)
            chosen = before_ref[span, :] if started else jnp.zeros((GROUP, tile), F32)
            for k in range(slots):
                chosen += jnp.where(edge == k, values[k * GROUP : (k + 1) * GROUP], 0.0)
            if not last:
                outs[0][span, :] = chosen
                return
            spread = jnp.zeros((rows, tile), F32)
            for _ in range(3):
                high = chosen.astype(BF16)
                chosen = chosen - high.astype(F32)
                spread += transposed_dot(own, high)
            total[:, pl.ds(at, tile)] += spread

        spread_prior(0)

        @pl.loop(0, jnp.minimum(units, BATCH))
        def _(u):
            one_unit(0, u, lambda i, u: near_ref[pl.ds(pl.multiple_of(u * UNIT, UNIT), UNIT), deep[i]])

        @pl.loop(1, (units + BATCH - 1) // BATCH)
        def _(c):
            here = jnp.minimum(units - c * BATCH, BATCH)

            @pl.loop(0, here)
            def _(u):
                for i in range(count):
                    look_copy(i, c, u).start()

            spread_prior(c)

            @pl.loop(0, here)
            def _(u):
                for i in range(count):
                    look_copy(i, c, u).wait()
                one_unit(c, u, lambda i, u: looks[i, u])

        if last:
            first = lax.axis_index("hid") * local if local < rows else 0
            outs[0][...] = total[pl.ds(pl.multiple_of(first, local), local), :]
            theirs = local - first if local < rows else 0
            outs[1][...] = total[pl.ds(pl.multiple_of(theirs, local), local), :].astype(BF16)
            sums = jnp.sum(total[...], axis=1, keepdims=True)
            outs[2][...] = jnp.broadcast_to(sums, (rows, 128)).T[0:1, :]

    if last:
        shapes = [((local, columns), F32), ((local, columns), BF16), ((1, rows), F32)]
    else:
        shapes = [((seats, tile), F32)]
    return pl.pallas_call(
        kernel,
        in_specs=[SMEM] + [VMEM] * len(arrays) + [VMEM, VMEM, HBM, VMEM, VMEM] + [VMEM] * started,
        out_specs=[VMEM] * len(shapes),
        scratch_shapes=[
            pltpu.VMEM((count, BATCH, UNIT, width), BF16),
            pltpu.VMEM((count, BATCH * GROUP, width), BF16),
            pltpu.VMEM((rows, columns), F32),
            pltpu.SemaphoreType.DMA((count, BATCH)),
        ],
        out_shape=[jax.ShapeDtypeStruct(*shape) for shape in shapes],
        compiler_params=params(12),
        cost_estimate=cheap(),
        name="piece_scores",
    )(head, *arrays, select, *look, emission, edges, *([before] if started else []))


def body(sizes, posterior, transition, emission, advance, dfa_state, edge_next, token_edge, allowed):
    vocab_size, hid_size = sizes
    rows = posterior.shape[0]
    hidden = transition.shape[1]
    slots = edge_next.shape[1]
    chips = vocab_size // 2
    width = hidden // vocab_size
    direct = chips == 8 and width % 128 == 0
    local = rows // hid_size
    first = lax.axis_index("hid") * local
    blocks = allowed.shape[1]
    tile = min(2, blocks) * BLK

    def swap(array, bits):
        return lax.ppermute(array, "vocab", [(i, i ^ bits) for i in range(vocab_size)])

    def seated(allowed, dfa_state, edge_next, token_edge):
        return take_seats(allowed.T, dfa_state[None, :], edge_next, in_hbm(token_edge), tile)

    small = (allowed, dfa_state, edge_next, token_edge)
    if direct:
        order = FAR_OTHER + FAR_SAME + NEAR_OTHER + NEAR_SAME
        away = half_product(posterior, transition, True, order, chips, width)
        came = swap(away, 1)
        kept = half_product(posterior, transition, False, order[:4], chips, width)
        parts = [(kept[n : n + 2].astype(F32) + came[n : n + 2].astype(F32)).astype(BF16) for n in (0, 2)]
        parts, posterior = lax.optimization_barrier((parts, posterior))
        far = swap(parts[0], 2)
        kept = half_product(posterior, transition, False, order[4:], chips, width)
        parts += [(kept[n : n + 2].astype(F32) + came[n + 4 : n + 6].astype(F32)).astype(BF16) for n in (0, 2)]
        parts, small = lax.optimization_barrier((parts, small))
        near = swap(parts[2], 2)
        head, select, after, edges = seated(*small)
        far, head, select, after, edges = lax.optimization_barrier((far, head, select, after, edges))
        far = parts[1].astype(F32) + far.astype(F32)
        sent = [swap(far[0].astype(BF16), 8), swap(far[1].astype(BF16), 12)]
        near = parts[3].astype(F32) + near.astype(F32)
        sent.append(swap(near[1].astype(BF16), 4))
        own = near[0] + sent[0].astype(F32) + sent[1].astype(F32) + sent[2].astype(F32)
        own = own.astype(BF16)

        own, head = lax.optimization_barrier((own, head))
        far = [swap(own, 8), swap(own, 12)]
        *look, emission = successor_rows(head, after, in_hbm(advance), in_hbm(emission))
        far, column, emission = lax.optimization_barrier((far, swap(own, 4), emission))
        far = jnp.stack(far)
        beside = swap(own, 2)
        near = jnp.stack([own, beside])

        def one_batch(arrays, bits, before, last):
            def places():
                groups = [bits[n : n + 2] for n in range(0, len(bits), 2)]
                return [piece_place(chips, other, b) for group in groups for other in (False, True) for b in group]

            arrays = [one for array in arrays for one in (array, swap(array, 1))]
            return piece_scores(
                arrays, places, head, select, look, emission, edges, before, slots, tile, last, local
            )

    else:
        own = lax.psum_scatter(
            jnp.dot(posterior, transition, preferred_element_type=F32), "vocab", scatter_dimension=0, tiled=True
        ).astype(BF16)
        prior = lax.all_gather(own, "vocab", axis=0, tiled=True)
        head, select, after, edges = seated(*small)
        *look, emission = successor_rows(head, after, in_hbm(advance), in_hbm(emission))
        wide = min(512, hidden)

        def one_batch(array, j, before, last):
            return piece_scores(
                [array], lambda: [j], head, select, look, emission, edges, before, slots, tile, last, rows
            )

    if direct:
        chosen = one_batch([near, far], (0, 1, 4, 6), None, False)[0]
        across, diagonal, chosen = lax.optimization_barrier((swap(far, 2), swap(beside, 4), chosen))
        got = one_batch([across, jnp.stack([column, diagonal])], (5, 7, 2, 3), chosen, True)
    else:
        chosen = None
        for j in range(hidden // wide):
            got = one_batch(prior[None, :, wide * j : wide * (j + 1)], j, chosen, j == hidden // wide - 1)
            chosen = got[0]
    mine, theirs, part = got

    if hid_size == 2:
        theirs = lax.ppermute(theirs, "hid", [(0, 1), (1, 0)])
        if direct:
            part = part + swap(part, 8) + swap(part, 12) + swap(part, 4)
            part = part + swap(part, 1)
            across = [(i, i ^ 5) for i in range(2 * vocab_size)]
            later = swap(part, 2) + lax.ppermute(part, ("vocab", "hid"), across)
            again, theirs = lax.optimization_barrier((part, theirs))
            part = part + lax.ppermute(again, "hid", [(0, 1), (1, 0)]) + later
        else:
            part = lax.psum(part, ("vocab", "hid"))
        totals = lax.dynamic_slice_in_dim(part[0], first, local, 0)
        mine = mine + theirs.astype(F32)
    else:
        mine = lax.psum_scatter(theirs, "hid", scatter_dimension=0, tiled=True).astype(F32)
        totals = lax.psum(jnp.sum(mine, axis=1), "vocab")
    mask = jnp.repeat(lax.dynamic_slice_in_dim(allowed, first, local, 0), BLK, axis=1) > 0
    safe = jnp.where(mask, mine, jnp.float32(1.0))
    return jnp.where(mask, jnp.log(safe) - jnp.log(totals)[:, None], jnp.float32(0.0))


def solution(mesh):
    in_specs = (
        P(None, "vocab"),
        P("vocab", "hid"),
        P("hid", "vocab"),
        P(None, "hid"),
        P(),
        P(),
        P(None, "vocab"),
        P(None, "vocab"),
    )
    sizes = (mesh.shape["vocab"], mesh.shape["hid"])
    return jax.shard_map(
        functools.partial(body, sizes), mesh=mesh, in_specs=in_specs, out_specs=P("hid", "vocab"), check_vma=False
    )
```
